1024 devices in a mesh: rep: 64 (over x, y), exp: 16 (over z, core).
Axes of the slice: x: 8, y: 8, z: 8, core: 2. Of those that a mesh axis runs over, the one named last changes fastest.
Arguments:
- x_rows: bfloat16 [64, 2048, 2048], P('rep', 'exp'), may hold values from -8 to 8
- row_cot: bfloat16 [64, 2048, 2048], P('rep', 'exp'), may hold values from -8 to 8
- gate_vals: float32 [64, 2048], P('rep', 'exp'), may hold values from 0 to 1, as said below
- route_pos: int32 [64, 320, 4], P('rep', 'exp'), may hold values from 0 to 127, as said below
- weights: bfloat16 [16, 3, 2048, 384], P('exp'), may hold values from -0.125 to 0.125
- momentum: float32 [16, 3, 2048, 384], P('exp', None, 'rep'), may hold values from -6 to 6
Outputs:
- token_grad: bfloat16 [64, 320, 2048], P('rep', 'exp')
- momentum_new: float32 [16, 3, 2048, 384], P('exp', None, 'rep')
The draws below stay inside these ranges and needn't reach their ends.
Inputs may be any that keep to these rules, and one draw needn't show every extreme that they name: `route_pos`: for each token of an owner, 4 positions e * 8 + c in ascending order, from 4 different experts e; from expert e an owner refers to slots c = 0 .. n - 1, each by exactly one token, where n is at most 8 and equals 8 for some expert of every owner; in every replica some owner uses all 8 slots of the last expert and some owner all of expert 0. `gate_vals`: row o * 8 + c of an expert in a replica belongs to owner o's slot c; its weight is zero exactly where no token of that owner refers to the slot, and positive elsewhere.
All inputs are finite; a program needn't handle non-finite values.
Results may differ from the reference program's by a relative error of at most 0.0064.
Values may be sent and summed in bfloat16 or wider, within the bound.
A program may use at most 64 MiB of HBM per device.

```python
import math
import jax
import jax.numpy as jnp
from jax import lax

D = 2048
FF = 384
TOPK = 4
ROWS = 128
REPLICAS = 64
EXPERTS = 16
CAP = 8
TOK_DEV = 20
LIMIT = 8


def owner_routes(owner_key, full_expert):
    key_score, key_order = jax.random.split(owner_key, 2)
    raw_score = jax.random.randint(key_score, (EXPERTS, LIMIT), 0, 1 << 14)
    slot_index = jnp.arange(EXPERTS * LIMIT, dtype=jnp.int32).reshape(EXPERTS, LIMIT)
    expert_index = jnp.arange(EXPERTS, dtype=jnp.int32)
    scores = raw_score * (EXPERTS * LIMIT) + slot_index
    scores = jnp.where(expert_index[:, None] == full_expert, -1 - slot_index, scores)
    unused, chosen = lax.top_k(-scores.reshape(-1), TOK_DEV * TOPK)
    picked = jnp.zeros((EXPERTS * LIMIT,), jnp.int32).at[chosen].set(1)
    counts = jnp.sum(picked.reshape(EXPERTS, LIMIT), axis=1)
    ends = jnp.cumsum(counts)
    starts = ends - counts
    order_pos = jnp.arange(TOK_DEV * TOPK, dtype=jnp.int32)
    expert_of = jnp.sum((order_pos[:, None] >= ends[None, :]).astype(jnp.int32), axis=1)
    start_of = jnp.sum(jnp.where(expert_index[None, :] == expert_of[:, None], starts[None, :], 0), axis=1)
    positions = expert_of * CAP + (order_pos - start_of)
    by_token = positions.reshape(TOPK, TOK_DEV).T
    shuffle = jax.random.permutation(key_order, TOK_DEV)
    routes = jnp.zeros((TOK_DEV, TOPK), jnp.int32).at[shuffle].set(by_token)
    return (routes, counts)


def all_routes(key):
    base = jax.random.fold_in(key, 7)
    keys = jax.random.split(base, REPLICAS * EXPERTS)
    shifts = jax.random.randint(jax.random.fold_in(base, 13), (REPLICAS,), 0, EXPERTS)
    owners = jnp.arange(EXPERTS, dtype=jnp.int32)
    full_experts = ((owners[None, :] + shifts[:, None]) % EXPERTS).reshape(-1).astype(jnp.int32)
    routes, counts = jax.vmap(owner_routes)(keys, full_experts)
    return (routes.reshape(REPLICAS, EXPERTS * TOK_DEV, TOPK), counts.reshape(REPLICAS, EXPERTS, EXPERTS))


def draw_route_pos(key, part):
    return all_routes(key)[0].astype(jnp.int32)


def draw_gate_vals(key, part):
    unused, counts = all_routes(key)
    slots = jnp.arange(CAP, dtype=jnp.int32)
    by_expert = jnp.transpose(counts, (0, 2, 1))
    live = (slots[None, None, None, :] < by_expert[:, :, :, None]).astype(jnp.float32)
    value_key = jax.random.fold_in(key, 11)
    shape = (REPLICAS, EXPERTS, EXPERTS, CAP)
    values = jnp.exp(jax.random.uniform(value_key, shape, jnp.float32, math.log(0.1), 0.0))
    return (values * live).reshape(REPLICAS, EXPERTS * ROWS).astype(jnp.float32)


def mixed_rows(key, salt, amp_lo, with_signs):
    base = jax.random.fold_in(key, salt)
    key_scale, key_shared, key_own, key_amp, key_sign, key_pick = jax.random.split(base, 6)
    count_rows = EXPERTS * ROWS
    block_count = REPLICAS
    block_width = D // REPLICAS
    amp_sq = jax.random.uniform(key_amp, (block_count,), jnp.float32, amp_lo, 0.95)
    amp_shared = jnp.sqrt(amp_sq)
    amp_own = jnp.sqrt(1.0 - amp_sq)
    if with_signs:
        flip_block = jnp.where(jax.random.uniform(key_pick, (block_count,), jnp.float32) < 0.5, 1.0, 0.0)
        coin = jnp.where(jax.random.uniform(key_sign, (REPLICAS, block_count), jnp.float32) < 0.5, 1.0, -1.0)
        signs = 1.0 - flip_block[None, :] * (1.0 - coin)
    else:
        signs = jnp.ones((REPLICAS, block_count), jnp.float32)
    shared_weight = jnp.repeat(signs * amp_shared[None, :], block_width, axis=1)
    own_weight = jnp.repeat(amp_own, block_width, axis=0)
    col_scale = jnp.exp(jax.random.uniform(key_scale, (D,), jnp.float32, math.log(0.3), math.log(3.0)))
    shared = jax.random.normal(key_shared, (count_rows, D), jnp.float32)
    own_part = jax.random.normal(key_own, (REPLICAS, count_rows, D), jnp.float32)
    mixed = shared[None] * shared_weight[:, None, :] + own_part * own_weight[None, None, :]
    return jnp.clip(mixed * col_scale[None, None, :] / 1.4, -8.0, 8.0)


def draw_x_rows(key, part):
    return mixed_rows(key, 3, 0.5, False).astype(jnp.bfloat16)


def draw_row_cot(key, part):
    return mixed_rows(key, 5, 0.3, True).astype(jnp.bfloat16)


def block_levels(stream_key, extent, shards, least, top_value):
    gain, own = 1.0, jax.random.fold_in(stream_key, 6)
    for dim, shards_of in shards:
        steps = jnp.exp(jax.random.uniform(jax.random.fold_in(own, dim), (shards_of,), jnp.float32, least / len(shards), top_value / len(shards)))
        gain = gain * jnp.repeat(steps, extent[dim] // shards_of).reshape([-1 if axis == dim else 1 for axis in range(len(extent))])
    return gain


def gaussian(key, dims, width, reach, pieces=(), held_as=jnp.bfloat16):
    result = jax.random.normal(key, dims, jnp.float32) * width
    if len(pieces) > 0:
        result = block_levels(key, dims, pieces, -0.22, 0.18) * result
    return jnp.clip(result, min=-reach, max=reach).astype(held_as)


def setup_inputs(seed: int = 0) -> dict:
    arg_keys = jax.random.split(jax.random.key(seed), 7)
    x_rows = draw_x_rows(jax.random.fold_in(arg_keys[6], 71), 0)
    row_cot = draw_row_cot(jax.random.fold_in(arg_keys[6], 71), 0)
    gate_vals = draw_gate_vals(jax.random.fold_in(arg_keys[6], 71), 0)
    route_pos = draw_route_pos(jax.random.fold_in(arg_keys[6], 71), 0)
    weights = gaussian(arg_keys[4], (EXPERTS, 3, D, FF), D ** -0.5, 0.125, ((0, 16),))
    momentum = gaussian(arg_keys[5], (EXPERTS, 3, D, FF), 1.0, 6.0, ((0, 16), (2, 64)), jnp.float32)
    return dict(x_rows=x_rows, row_cot=row_cot, gate_vals=gate_vals, route_pos=route_pos, weights=weights, momentum=momentum)


tiny_eps = 1e-6
moment_decay = 0.9


def expert_backward(routed, out_cot, gate_row, w_gate, w_up, w_down_t):
    gate_pre = jnp.dot(routed, w_gate, preferred_element_type=jnp.float32)
    up_pre = jnp.dot(routed, w_up, preferred_element_type=jnp.float32)
    sigma_gate = jax.nn.sigmoid(gate_pre)
    activation = gate_pre * sigma_gate
    hidden = (activation * up_pre).astype(jnp.bfloat16)
    scaled = (gate_row[:, None] * out_cot.astype(jnp.float32)).astype(jnp.bfloat16)
    contract_rows = (((0,), (0,)), ((), ()))
    down_grad = lax.dot_general(scaled, hidden, contract_rows, preferred_element_type=jnp.float32)
    hidden_grad = jnp.dot(scaled, w_down_t, preferred_element_type=jnp.float32)
    gate_grad = (hidden_grad * up_pre * sigma_gate * (1.0 + gate_pre * (1.0 - sigma_gate))).astype(jnp.bfloat16)
    up_grad = (hidden_grad * activation).astype(jnp.bfloat16)
    contract_cols = (((1,), (1,)), ((), ()))
    row_grad = lax.dot_general(gate_grad, w_gate, contract_cols, preferred_element_type=jnp.float32)
    row_grad = row_grad + lax.dot_general(up_grad, w_up, contract_cols, preferred_element_type=jnp.float32)
    grad_gate = lax.dot_general(routed, gate_grad, contract_rows, preferred_element_type=jnp.float32)
    grad_up = lax.dot_general(routed, up_grad, contract_rows, preferred_element_type=jnp.float32)
    grad_stack = jnp.stack([grad_gate, grad_up, down_grad], axis=0).astype(jnp.bfloat16)
    return grad_stack, row_grad.astype(jnp.bfloat16)


def adasum_tree(grads):
    levels = REPLICAS.bit_length() - 1
    current = grads
    for section in range(levels):
        count = current.shape[0] // 2
        first_part = current[:count].astype(jnp.float32)
        second_part = current[count:].astype(jnp.float32)
        inner = jnp.sum(first_part * second_part, axis=(2, 3))
        first_sq = jnp.sum(first_part * first_part, axis=(2, 3))
        second_sq = jnp.sum(second_part * second_part, axis=(2, 3))
        coef_first = 1.0 - inner / (2.0 * (first_sq + tiny_eps))
        coef_second = 1.0 - inner / (2.0 * (second_sq + tiny_eps))
        merged = coef_first[:, :, None, None] * first_part + coef_second[:, :, None, None] * second_part
        if section == levels - 1:
            current = merged
        else:
            current = merged.astype(jnp.bfloat16)
    return current[0]


def reference(x_rows, row_cot, gate_vals, route_pos, weights, momentum):
    by_expert_x = x_rows.reshape(REPLICAS, EXPERTS, ROWS, D).transpose(1, 0, 2, 3)
    by_expert_c = row_cot.reshape(REPLICAS, EXPERTS, ROWS, D).transpose(1, 0, 2, 3)
    by_expert_g = gate_vals.reshape(REPLICAS, EXPERTS, ROWS).transpose(1, 0, 2)

    def per_expert(operands):
        xs_expert, cs_expert, gs_expert, w_expert = operands

        def per_replica(inner):
            return expert_backward(inner[0], inner[1], inner[2], w_expert[0], w_expert[1], w_expert[2])

        grads, row_grads = lax.map(per_replica, (xs_expert, cs_expert, gs_expert))
        return adasum_tree(grads), row_grads

    combined, row_grads = lax.map(per_expert, (by_expert_x, by_expert_c, by_expert_g, weights))
    received = row_grads.reshape(EXPERTS, REPLICAS, EXPERTS, CAP, D).transpose(1, 2, 0, 3, 4)
    received = received.reshape(REPLICAS, EXPERTS, EXPERTS * CAP, D)
    routes = route_pos.reshape(REPLICAS, EXPERTS, TOK_DEV, TOPK)

    def gather_owner(recv_rows, indices):
        return jnp.sum(recv_rows[indices].astype(jnp.float32), axis=1)

    def per_replica_tokens(operands):
        return jax.vmap(gather_owner)(operands[0], operands[1])

    tokens = lax.map(per_replica_tokens, (received, routes))
    token_grad = tokens.reshape(REPLICAS, EXPERTS * TOK_DEV, D).astype(jnp.bfloat16)
    momentum_new = moment_decay * momentum + (1.0 - moment_decay) * combined
    return token_grad, momentum_new
```

```python
import functools
import math

import jax
import jax.numpy as jnp
from jax import lax
from jax.experimental import pallas as pl
from jax.experimental.pallas import tpu as pltpu
from jax.sharding import PartitionSpec as P

MESH = pl.DeviceIdType.MESH
tiny_eps = 1e-06
moment_decay = 0.9
ROWS_FIRST = (((0,), (0,)), ((), ()))
COLS_LAST = (((1,), (1,)), ((), ()))
f32 = jnp.float32
bf16 = jnp.bfloat16


def tile_iotas():
    sub = lax.broadcasted_iota(jnp.int32, (8, 128), 0)
    lane = lax.broadcasted_iota(jnp.int32, (8, 128), 1)
    return sub, lane


def gram_tile(read, n, rows, cols, rows_buf):
    pairs = [(k, l) for k in range(n) for l in range(k, n)]

    def body(i, accs):
        row = pl.multiple_of(i * 8, 8)
        accs = list(accs)
        for c in range(cols // 128):
            vals = [read(k, row, c * 128) for k in range(n)]
            for at, (k, l) in enumerate(pairs):
                accs[at] = accs[at] + vals[k] * vals[l]
        return tuple(accs)

    zero = jnp.zeros((8, 128), f32)
    accs = lax.fori_loop(0, rows // 8, body, tuple(zero for _ in pairs))
    for (k, l), acc in zip(pairs, accs):
        total = jnp.sum(acc, axis=0, keepdims=True)
        for a in range(8):
            for b in range(8):
                if sorted((a % n, b % n)) == [k, l]:
                    rows_buf[a * 8 + b : a * 8 + b + 1, :] = total
    sub, lane = tile_iotas()
    tile = zero
    for b in range(8):
        col = jnp.sum(rows_buf[b * 8 : b * 8 + 8, :], axis=1, keepdims=True)
        tile = tile + jnp.where((lane & 7) == b, col, 0.0)
    return tile


def tree_weights(tile, n):
    sub, lane = tile_iotas()
    weights = jnp.ones((8, 128), f32)
    half = n // 2
    while half >= 1:
        other = (sub + half) & 7
        here_c = jnp.where(lane == sub, tile, 0.0)
        there_c = jnp.where(lane == other, tile, 0.0)
        here_r = jnp.where((lane & 7) == sub, tile, 0.0)
        there_r = jnp.where((lane & 7) == other, tile, 0.0)
        q_col = jnp.maximum(jnp.sum(here_c, axis=1, keepdims=True), 0.0)
        p_col = jnp.sum(there_c, axis=1, keepdims=True)
        q_row = jnp.maximum(jnp.sum(here_r, axis=0, keepdims=True), 0.0)
        p_row = jnp.sum(there_r, axis=0, keepdims=True)
        q_col_b = jnp.broadcast_to(q_col, (8, 128))
        q_row_b = jnp.broadcast_to(q_row, (8, 128))
        most_c = jnp.sqrt(q_col_b) * jnp.sqrt(pltpu.roll(q_col_b, half, 0))
        most_r = jnp.sqrt(q_row_b) * jnp.sqrt(pltpu.roll(q_row_b, half, 1))
        p_col_b = jnp.clip(jnp.broadcast_to(p_col, (8, 128)), -most_c, most_c)
        p_row_b = jnp.clip(jnp.broadcast_to(p_row, (8, 128)), -most_r, most_r)
        coef_c = 1.0 - p_col_b / (2.0 * (q_col_b + tiny_eps))
        coef_r = 1.0 - p_row_b / (2.0 * (q_row_b + tiny_eps))
        weights = weights * coef_c
        tile = tile * coef_c * coef_r
        tile = tile + pltpu.roll(tile, half, 0)
        tile = tile + pltpu.roll(tile, half, 1)
        half //= 2
    return weights


def summed_tiles(buf, n, shifted):
    total = buf[0]
    for j in range(1, n):
        tile = buf[j]
        if shifted:
            tile = pltpu.roll(pltpu.roll(tile, j, 0), j, 1)
        total = total + tile
    return total


def kernel(
    nx, ny, ne,
    x_ref, cot_ref, gate_ref, route_ref, w_ref,
    token_ref, comb_ref,
    cot_v, w_v, xs, ss, xr, sr, a_buf, g_buf, zs, zr,
    c3, yr, yf, st1, st2, st3, rows_buf, wt_buf,
    load_sem, x_sem, xsend, xrecv, asend, arecv, zsend, zrecv,
    ysend, yrecv, s1send, s1recv, s2send, s2recv, s3send, s3recv,
):
    rep = lax.axis_index("rep")
    me_e = lax.axis_index("exp")
    me_x = lax.div(rep, ny)
    me_y = lax.rem(rep, ny)
    rows, width = cot_v.shape
    ff = w_v.shape[2]
    dx = width // nx
    dy = dx // ny
    half_w = width // 2

    def x_peer(k):
        return (lax.rem(me_x + k, nx) * ny + me_y, me_e)

    def y_peer(k):
        return (me_x * ny + lax.rem(me_y + k, ny), me_e)

    def e_peer(k):
        return (rep, lax.rem(me_e + k, ne))

    cot_load = pltpu.make_async_copy(cot_ref.at[0], cot_v, load_sem.at[0])
    cot_load.start()
    x_loads = []
    for j in range(nx):
        load = pltpu.make_async_copy(x_ref.at[0, :, pl.ds(j * dx, dx)], xs.at[j], x_sem.at[j])
        load.start()
        x_loads.append(load)
    w_loads = []
    for t in range(3):
        load = pltpu.make_async_copy(w_ref.at[0, t], w_v.at[t], load_sem.at[1 + t])
        load.start()
        w_loads.append(load)

    barrier = pltpu.get_barrier_semaphore()
    peers = [x_peer(k) for k in range(1, nx)]
    peers += [y_peer(k) for k in range(1, ny)]
    peers += [e_peer(k) for k in range(1, ne)]
    for peer in peers:
        pl.semaphore_signal(barrier, inc=1, device_id=peer, device_id_type=MESH)

    eye = lax.broadcasted_iota(jnp.int32, (rows, rows), 0) == lax.broadcasted_iota(
        jnp.int32, (rows, rows), 1
    )
    gate_col = jnp.sum(jnp.where(eye, gate_ref[...], 0.0), axis=1, keepdims=True)
    cot_load.wait()
    for j in range(nx):
        ss[j] = (gate_col * cot_v[:, j * dx : (j + 1) * dx].astype(f32)).astype(bf16)

    if peers:
        pl.semaphore_wait(barrier, len(peers))

    def send(src, dst, ssem, rsem, peer):
        copy = pltpu.make_async_remote_copy(
            src_ref=src, dst_ref=dst, send_sem=ssem, recv_sem=rsem,
            device_id=peer, device_id_type=MESH,
        )
        copy.start()

    def wait_bytes(ref, sem):
        pltpu.make_async_copy(ref, ref, sem).wait()

    order_x = sorted(range(1, nx), key=lambda k: -min(k, nx - k))
    order_y = sorted(range(1, ny), key=lambda k: -min(k, ny - k))

    for k in order_x:
        send(ss.at[lax.rem(me_x + k, nx)], sr.at[nx - k], xsend.at[0], xrecv.at[0], x_peer(k))
    sr[0] = ss[me_x]
    for load in x_loads:
        load.wait()
    for k in order_x:
        send(xs.at[lax.rem(me_x + k, nx)], xr.at[nx - k], xsend.at[1], xrecv.at[1], x_peer(k))
    xr[0] = xs[me_x]

    far = nx // 2

    def ring_parts(step):
        parts = []
        if step < far:
            parts.append(((nx - step + 1) % nx, nx - step, 0, rows, 1))
            parts.append((step - 1, step, 0, rows, nx - 1))
        else:
            parts.append(((nx - step + 1) % nx, far, 0, rows // 2, 1))
            parts.append((step - 1, far, rows // 2, rows // 2, nx - 1))
        return parts

    def ring_refs(t, step):
        found = []
        for way, (src, dst, first, count, offset) in enumerate(ring_parts(step)):
            found.append((
                a_buf.at[t, src, pl.ds(first, count)],
                a_buf.at[t, dst, pl.ds(first, count)],
                (t * far + step - 1) * 2 + way,
                offset,
            ))
        return found

    def ring_wait(t, step):
        for src, dst, at, offset in ring_refs(t, step):
            wait_bytes(dst, arecv.at[at])

    def ring_step(t, step):
        if step > 1:
            ring_wait(t, step - 1)
        for src, dst, at, offset in ring_refs(t, step):
            send(src, dst, asend.at[at], arecv.at[at], x_peer(offset))

    w_loads[0].wait()
    w_loads[1].wait()
    gate_pre = jnp.zeros((rows, ff), f32)
    up_pre = jnp.zeros((rows, ff), f32)
    for j in range(nx):
        part = xs[j]
        gate_pre += jnp.dot(part, w_v[0, j * dx : (j + 1) * dx, :], preferred_element_type=f32)
        up_pre += jnp.dot(part, w_v[1, j * dx : (j + 1) * dx, :], preferred_element_type=f32)
    sigma = 1.0 / (1.0 + jnp.exp(-gate_pre))
    act = gate_pre * sigma
    a_buf[0, 0] = (act * up_pre).astype(bf16)
    ring_step(0, 1)

    w_loads[2].wait()
    hidden_grad = jnp.zeros((rows, ff), f32)
    for j in range(nx):
        hidden_grad += jnp.dot(ss[j], w_v[2, j * dx : (j + 1) * dx, :], preferred_element_type=f32)
    a_buf[1, 0] = (hidden_grad * up_pre * sigma * (1.0 + gate_pre * (1.0 - sigma))).astype(bf16)
    ring_step(1, 1)
    a_buf[2, 0] = (hidden_grad * act).astype(bf16)
    ring_step(2, 1)

    def row_grads():
        gate_grad = a_buf[1, 0]
        up_grad = a_buf[2, 0]
        blk = min(256, half_w)

        def piece(col):
            at = pl.ds(pl.multiple_of(col, blk), blk)
            val = lax.dot_general(gate_grad, w_v[0, at, :], COLS_LAST, preferred_element_type=f32)
            val += lax.dot_general(up_grad, w_v[1, at, :], COLS_LAST, preferred_element_type=f32)
            return val.reshape(ne, rows // ne, blk)

        def body(j, carry):
            both = jnp.concatenate([piece(j * blk), piece(half_w + j * blk)], axis=1)
            zs[:, :, pl.ds(pl.multiple_of(j * blk, blk), blk)] = both.astype(bf16)
            return carry

        lax.fori_loop(0, half_w // blk, body, 0)
        for k in range(1, ne):
            send(zs.at[lax.rem(me_e + k, ne)], zr.at[ne - k], zsend.at[0], zrecv.at[0], e_peer(k))
        zr[0] = zs[me_e]

    def tokens():
        wait_bytes(zr.at[pl.ds(1, ne - 1)], zrecv.at[0])
        cap = rows // ne
        tall = ne * 2 * cap
        count = token_ref.shape[1]
        route = route_ref[0]
        at = ((lax.div(route, cap) - me_e + ne) & (ne - 1)) * (2 * cap) + lax.rem(route, cap)
        col = lax.broadcasted_iota(jnp.int32, (count, tall), 1)
        low = jnp.zeros((count, tall), f32)
        high = jnp.zeros((count, tall), f32)
        for k in range(route.shape[1]):
            low += jnp.where(col == at[:, k : k + 1], 1.0, 0.0)
            high += jnp.where(col == at[:, k : k + 1] + cap, 1.0, 0.0)
        got = zr[...].reshape(tall, half_w)
        token_ref[0, :, :half_w] = jnp.dot(low.astype(bf16), got, preferred_element_type=f32)
        token_ref[0, :, half_w:] = jnp.dot(high.astype(bf16), got, preferred_element_type=f32)

    def combine_1(t):
        left = sr if t == 0 else xr

        def body(k, carry):
            g_buf[t, k] = lax.dot_general(left[k], a_buf[t, k], ROWS_FIRST, preferred_element_type=f32)
            return carry

        lax.fori_loop(0, nx, body, 0)

        def read(k, row, col):
            return g_buf[t, k, pl.ds(row, 8), col : col + 128]

        st1[t, 0] = gram_tile(read, nx, dx, ff, rows_buf)
        for k in order_x:
            send(st1.at[t, 0], st1.at[t, nx - k], s1send.at[t], s1recv.at[t], x_peer(k))

    def combine_2(t):
        wait_bytes(st1.at[t, pl.ds(1, nx - 1)], s1recv.at[t])
        wt_buf[...] = tree_weights(summed_tiles(st1.at[t], nx, True), nx)
        lanes = [wt_buf[k : k + 1, :] for k in range(nx)]

        def body(i, carry):
            at = pl.ds(pl.multiple_of(i * 16, 16), 16)
            for c in range(ff // 128):
                cols = slice(c * 128, c * 128 + 128)
                total = lanes[0] * g_buf[t, 0, at, cols]
                for k in range(1, nx):
                    total = total + lanes[k] * g_buf[t, k, at, cols]
                c3[t, at, cols] = total.astype(bf16)
            return carry

        lax.fori_loop(0, dx // 16, body, 0)
        for k in order_y:
            first = pl.multiple_of(lax.rem(me_y + k, ny) * dy, dy)
            send(c3.at[t, pl.ds(first, dy)], yr.at[t, ny - k], ysend.at[t], yrecv.at[t], y_peer(k))
        yr[t, 0] = c3[t, pl.ds(pl.multiple_of(me_y * dy, dy), dy)]

    def combine_3(t):
        wait_bytes(yr.at[t, pl.ds(1, ny - 1)], yrecv.at[t])
        yf[t] = yr[t].astype(f32)

        def read(k, row, col):
            return yf[t, k, pl.ds(row, 8), col : col + 128]

        st2[t, 0] = gram_tile(read, ny, dy, ff, rows_buf)
        for k in order_x:
            send(st2.at[t, 0], st2.at[t, nx - k], s2send.at[t], s2recv.at[t], x_peer(k))

    def combine_4(t):
        wait_bytes(st2.at[t, pl.ds(1, nx - 1)], s2recv.at[t])
        st3[t, 0] = summed_tiles(st2.at[t], nx, False)
        for k in order_y:
            send(st3.at[t, 0], st3.at[t, ny - k], s3send.at[t], s3recv.at[t], y_peer(k))

    def combine_5(t):
        wait_bytes(st3.at[t, pl.ds(1, ny - 1)], s3recv.at[t])
        wt_buf[...] = tree_weights(summed_tiles(st3.at[t], ny, True), ny)
        for c in range(ff // 128):
            cols = slice(c * 128, c * 128 + 128)
            total = wt_buf[0:1, :] * yf[t, 0, :, cols]
            for k in range(1, ny):
                total = total + wt_buf[k : k + 1, :] * yf[t, k, :, cols]
            comb_ref[(t + 2) % 3, :, cols] = total

    def ready(t):
        ring_wait(t, far)
        if t < 2:
            wait_bytes((sr, xr)[t].at[pl.ds(1, nx - 1)], xrecv.at[t])

    ring_step(0, 2)
    row_grads()
    for step in range(2, far + 1):
        for t in range(3):
            if (t, step) != (0, 2):
                ring_step(t, step)
    tokens()
    ready(0)
    combine_1(0)
    ready(1)
    combine_1(1)
    combine_2(0)
    ready(2)
    combine_1(2)
    combine_2(1)
    combine_3(0)
    combine_2(2)
    combine_3(1)
    combine_4(0)
    combine_3(2)
    combine_4(1)
    combine_5(0)
    combine_4(2)
    combine_5(1)
    combine_5(2)

    for t, ref in enumerate((sr, xr)):
        wait_bytes(ref.at[pl.ds(1, nx - 1)], xsend.at[t])
    for t in range(3):
        for step in range(1, far + 1):
            for src, dst, at, offset in ring_refs(t, step):
                wait_bytes(src, asend.at[at])
        wait_bytes(st1.at[t, pl.ds(1, nx - 1)], s1send.at[t])
        wait_bytes(yr.at[t, pl.ds(1, ny - 1)], ysend.at[t])
        wait_bytes(st2.at[t, pl.ds(1, nx - 1)], s2send.at[t])
        wait_bytes(st3.at[t, pl.ds(1, ny - 1)], s3send.at[t])
    wait_bytes(zr.at[pl.ds(1, ne - 1)], zsend.at[0])


def on_device(nx, ny, ne, x_rows, row_cot, gate_vals, route_pos, weights, momentum):
    rows, width = x_rows.shape[1:]
    ff = weights.shape[3]
    dx = width // nx
    dy = dx // ny
    far = nx // 2
    tokens = route_pos.shape[1]
    vmem = pltpu.VMEM
    dma = pltpu.SemaphoreType.DMA
    in_hbm = pl.BlockSpec(memory_space=pl.ANY)
    in_vmem = pl.BlockSpec(memory_space=pltpu.VMEM)
    token_sum, combined = pl.pallas_call(
        functools.partial(kernel, nx, ny, ne),
        out_shape=(
            jax.ShapeDtypeStruct((1, tokens, width), f32),
            jax.ShapeDtypeStruct((3, dy, ff), f32),
        ),
        in_specs=[in_hbm, in_hbm, in_vmem, in_vmem, in_hbm],
        out_specs=(in_vmem, in_vmem),
        scratch_shapes=[
            vmem((rows, width), bf16),
            vmem((3, width, ff), bf16),
            vmem((nx, rows, dx), bf16),
            vmem((nx, rows, dx), bf16),
            vmem((nx, rows, dx), bf16),
            vmem((nx, rows, dx), bf16),
            vmem((3, nx, rows, ff), bf16),
            vmem((3, nx, dx, ff), f32),
            vmem((ne, 2 * rows // ne, width // 2), bf16),
            vmem((ne, 2 * rows // ne, width // 2), bf16),
            vmem((3, dx, ff), bf16),
            vmem((3, ny, dy, ff), bf16),
            vmem((3, ny, dy, ff), f32),
            vmem((3, nx, 8, 128), f32),
            vmem((3, nx, 8, 128), f32),
            vmem((3, ny, 8, 128), f32),
            vmem((64, 128), f32),
            vmem((8, 128), f32),
            dma((4,)),
            dma((nx,)),
            dma((2,)),
            dma((2,)),
            dma((6 * far,)),
            dma((6 * far,)),
            dma((1,)),
            dma((1,)),
            dma((3,)),
            dma((3,)),
            dma((3,)),
            dma((3,)),
            dma((3,)),
            dma((3,)),
            dma((3,)),
            dma((3,)),
        ],
        compiler_params=pltpu.CompilerParams(
            collective_id=0, has_side_effects=True, vmem_limit_bytes=56 * 1024 * 1024
        ),
        cost_estimate=pl.CostEstimate(
            flops=16 * rows * width * ff, bytes_accessed=2 * (3 * width * ff + 2 * rows * width),
            transcendentals=rows * ff,
        ),
    )(x_rows, row_cot, gate_vals, route_pos, weights)
    token_grad = token_sum.astype(bf16)
    momentum_new = moment_decay * momentum + (1.0 - moment_decay) * combined[None]
    return (token_grad, momentum_new)


def solution(mesh):
    reps, ne = mesh.shape["rep"], mesh.shape["exp"]
    nx = 1 << ((reps.bit_length()) // 2)
    ny = reps // nx
    placed = (
        P("rep", "exp", None),
        P("rep", "exp", None),
        P("rep", "exp"),
        P("rep", "exp", None),
        P("exp", None, None, None),
        P("exp", None, "rep", None),
    )
    return jax.shard_map(
        functools.partial(on_device, nx, ny, ne),
        mesh=mesh,
        in_specs=placed,
        out_specs=(P("rep", "exp", None), P("exp", None, "rep", None)),
        check_vma=False,
    )
```

```python
import functools
import math

import jax
import jax.numpy as jnp
from jax import lax
from jax.experimental import pallas as pl
from jax.experimental.pallas import tpu as pltpu
from jax.sharding import PartitionSpec as P

MESH = pl.DeviceIdType.MESH
tiny_eps = 1e-06
moment_decay = 0.9
ROWS_FIRST = (((0,), (0,)), ((), ()))
COLS_LAST = (((1,), (1,)), ((), ()))
f32 = jnp.float32
bf16 = jnp.bfloat16


def tile_iotas():
    sub = lax.broadcasted_iota(jnp.int32, (8, 128), 0)
    lane = lax.broadcasted_iota(jnp.int32, (8, 128), 1)
    return sub, lane


def gram_pairs(read, pairs, n, rows, cols, rows_buf):
    used = sorted({k for pair in pairs for k in pair})

    def body(i, accs):
        row = pl.multiple_of(i * 8, 8)
        accs = list(accs)
        for c in range(cols // 128):
            vals = {k: read(k, row, c * 128) for k in used}
            for at, (k, l) in enumerate(pairs):
                accs[at] = accs[at] + vals[k] * vals[l]
        return tuple(accs)

    zero = jnp.zeros((8, 128), f32)
    accs = lax.fori_loop(0, rows // 8, body, tuple(zero for _ in pairs))
    for (k, l), acc in zip(pairs, accs):
        total = jnp.sum(acc, axis=0, keepdims=True)
        for a in range(8):
            for b in range(8):
                if {a % n, b % n} == {k, l}:
                    rows_buf[a * 8 + b : a * 8 + b + 1, :] = total


def gram_tile(rows_buf):
    sub, lane = tile_iotas()
    tile = jnp.zeros((8, 128), f32)
    for b in range(8):
        col = jnp.sum(rows_buf[b * 8 : b * 8 + 8, :], axis=1, keepdims=True)
        tile = tile + jnp.where((lane & 7) == b, col, 0.0)
    return tile


def tree_weights(tile, n):
    sub, lane = tile_iotas()
    weights = jnp.ones((8, 128), f32)
    half = n // 2
    while half >= 1:
        other = (sub + half) & 7
        here_c = jnp.where(lane == sub, tile, 0.0)
        there_c = jnp.where(lane == other, tile, 0.0)
        here_r = jnp.where((lane & 7) == sub, tile, 0.0)
        there_r = jnp.where((lane & 7) == other, tile, 0.0)
        q_col = jnp.maximum(jnp.sum(here_c, axis=1, keepdims=True), 0.0)
        p_col = jnp.sum(there_c, axis=1, keepdims=True)
        q_row = jnp.maximum(jnp.sum(here_r, axis=0, keepdims=True), 0.0)
        p_row = jnp.sum(there_r, axis=0, keepdims=True)
        q_col_b = jnp.broadcast_to(q_col, (8, 128))
        q_row_b = jnp.broadcast_to(q_row, (8, 128))
        most_c = jnp.sqrt(q_col_b) * jnp.sqrt(pltpu.roll(q_col_b, half, 0))
        most_r = jnp.sqrt(q_row_b) * jnp.sqrt(pltpu.roll(q_row_b, half, 1))
        p_col_b = jnp.clip(jnp.broadcast_to(p_col, (8, 128)), -most_c, most_c)
        p_row_b = jnp.clip(jnp.broadcast_to(p_row, (8, 128)), -most_r, most_r)
        coef_c = 1.0 - p_col_b / (2.0 * (q_col_b + tiny_eps))
        coef_r = 1.0 - p_row_b / (2.0 * (q_row_b + tiny_eps))
        weights = weights * coef_c
        tile = tile * coef_c * coef_r
        tile = tile + pltpu.roll(tile, half, 0)
        tile = tile + pltpu.roll(tile, half, 1)
        half //= 2
    return weights


def summed_tiles(buf, at, n, shifted):
    total = buf[0, at]
    for j in range(1, n):
        tile = buf[j, at]
        if shifted:
            tile = pltpu.roll(pltpu.roll(tile, j, 0), j, 1)
        total = total + tile
    return total


def finish(token_ref, comb_ref, mom_ref, token_out, mom_out):
    token_out[...] = token_ref[...].astype(bf16)
    mom_out[0] = moment_decay * mom_ref[0] + (1.0 - moment_decay) * comb_ref[...]


def kernel(
    nx, ny, ne,
    x_ref, cot_ref, gate_ref, route_ref, w_ref,
    token_ref, comb_ref,
    cot_v, gate_v, route_v, w_v, xs, ss, xr, sr, a_buf, g_buf, zs, zr,
    c3_a, c3_b, yr_a, yr_b, yf, st1_a, st1_b, st2_a, st2_b, st3_a, st3_b, rows_buf, wt_buf,
    load_sem, x_sem, xsend, xrecv, asend, arecv, zsend, zrecv,
    ysend, yrecv, s1send, s1recv, s2send, s2recv, s3send, s3recv, near_sem,
):
    rep = lax.axis_index("rep")
    me_e = lax.axis_index("exp")
    me_x = lax.div(rep, ny)
    me_y = lax.rem(rep, ny)
    rows, width = cot_v.shape
    ff = w_v.shape[2]
    dx = width // nx
    dy = dx // ny
    half_w = width // 2
    far = nx // 2

    def x_peer(k):
        return (lax.rem(me_x + k, nx) * ny + me_y, me_e)

    def y_peer(k):
        return (me_x * ny + lax.rem(me_y + k, ny), me_e)

    def e_peer(k):
        return (rep, lax.rem(me_e + k, ne))

    chips = ne // 2
    chip = lax.div(me_e, 2)
    place = jnp.where(lax.rem(me_e, 2) == 0, chip, ne - 1 - chip)

    def on_line(at):
        return (rep, jnp.where(at < chips, 2 * at, 2 * (ne - 1 - at) + 1))

    def line_signal(sem, reach):
        @pl.when(place >= reach)
        def _():
            pl.semaphore_signal(sem, inc=1, device_id=on_line(place - reach), device_id_type=MESH)

        @pl.when(place + reach < ne)
        def _():
            pl.semaphore_signal(sem, inc=1, device_id=on_line(place + reach), device_id_type=MESH)

    def line_count(reach):
        return (place >= reach).astype(jnp.int32) + (place + reach < ne).astype(jnp.int32)

    cot_load = pltpu.make_async_copy(cot_ref.at[0], cot_v, load_sem.at[0])
    cot_load.start()
    gate_load = pltpu.make_async_copy(gate_ref, gate_v, load_sem.at[4])
    gate_load.start()
    x_loads = []
    for j in range(nx):
        load = pltpu.make_async_copy(x_ref.at[0, :, pl.ds(j * dx, dx)], xs.at[j], x_sem.at[j])
        load.start()
        x_loads.append(load)
    w_loads = []
    for t in range(3):
        load = pltpu.make_async_copy(w_ref.at[0, t], w_v.at[t], load_sem.at[1 + t])
        load.start()
        w_loads.append(load)
    route_load = pltpu.make_async_copy(route_ref, route_v, load_sem.at[5])
    route_load.start()

    barrier = pltpu.get_barrier_semaphore()
    peers = [x_peer(k) for k in range(1, nx)]
    peers += [y_peer(k) for k in range(1, ny)]
    for peer in peers:
        pl.semaphore_signal(barrier, inc=1, device_id=peer, device_id_type=MESH)

    line_signal(barrier, 1)

    eye = lax.broadcasted_iota(jnp.int32, (rows, rows), 0) == lax.broadcasted_iota(
        jnp.int32, (rows, rows), 1
    )
    cot_load.wait()
    gate_load.wait()
    gate_col = jnp.sum(jnp.where(eye, gate_v[...], 0.0), axis=1, keepdims=True)
    for j in range(nx):
        ss[j] = (gate_col * cot_v[:, j * dx : (j + 1) * dx].astype(f32)).astype(bf16)

    for load in x_loads:
        load.wait()
    w_loads[0].wait()
    w_loads[1].wait()
    gate_pre = jnp.zeros((rows, ff), f32)
    up_pre = jnp.zeros((rows, ff), f32)
    for j in range(nx):
        part = xs[j]
        gate_pre += jnp.dot(part, w_v[0, j * dx : (j + 1) * dx, :], preferred_element_type=f32)
        up_pre += jnp.dot(part, w_v[1, j * dx : (j + 1) * dx, :], preferred_element_type=f32)
    sigma = 1.0 / (1.0 + jnp.exp(-gate_pre))
    act = gate_pre * sigma
    a_buf[0, 0] = (act * up_pre).astype(bf16)
    w_loads[2].wait()
    hidden_grad = jnp.zeros((rows, ff), f32)
    for j in range(nx):
        hidden_grad += jnp.dot(ss[j], w_v[2, j * dx : (j + 1) * dx, :], preferred_element_type=f32)
    a_buf[1, 0] = (hidden_grad * up_pre * sigma * (1.0 + gate_pre * (1.0 - sigma))).astype(bf16)
    a_buf[2, 0] = (hidden_grad * act).astype(bf16)
    sr[0] = ss[me_x]
    xr[0] = xs[me_x]

    pl.semaphore_wait(barrier, len(peers) + line_count(1))

    def send(src, dst, ssem, rsem, peer):
        copy = pltpu.make_async_remote_copy(
            src_ref=src, dst_ref=dst, send_sem=ssem, recv_sem=rsem,
            device_id=peer, device_id_type=MESH,
        )
        copy.start()

    def wait_bytes(ref, sem):
        pltpu.make_async_copy(ref, ref, sem).wait()

    order_x = sorted(range(1, nx), key=lambda k: -min(k, nx - k))
    order_y = sorted(range(1, ny), key=lambda k: -min(k, ny - k))

    def ring_parts(step):
        parts = []
        if step < far:
            parts.append(((nx - step + 1) % nx, nx - step, 0, rows, 1))
            parts.append((step - 1, step, 0, rows, nx - 1))
        else:
            parts.append(((nx - step + 1) % nx, far, 0, rows // 2, 1))
            parts.append((step - 1, far, rows // 2, rows // 2, nx - 1))
        return parts

    def ring_refs(t, step):
        found = []
        for way, (src, dst, first, count, offset) in enumerate(ring_parts(step)):
            found.append((
                a_buf.at[t, src, pl.ds(first, count)],
                a_buf.at[t, dst, pl.ds(first, count)],
                (t * far + step - 1) * 2 + way,
                offset,
            ))
        return found

    def ring_wait(t, step):
        for src, dst, at, offset in ring_refs(t, step):
            wait_bytes(dst, arecv.at[at])

    def ring_step(t, step):
        if step > 1:
            ring_wait(t, step - 1)
        for src, dst, at, offset in ring_refs(t, step):
            send(src, dst, asend.at[at], arecv.at[at], x_peer(offset))

    nearest = []
    for k in range(1, far):
        nearest += [k, nx - k]
    nearest.append(far)
    cuts = (0, (len(nearest) + 1) * 3 // 8, (len(nearest) + 1) * 5 // 8, len(nearest))

    def send_left(t, piece):
        mine, there = (ss, sr) if t == 0 else (xs, xr)
        for k in nearest[cuts[piece] : cuts[piece + 1]]:
            send(mine.at[lax.rem(me_x + k, nx)], there.at[nx - k], xsend.at[t], xrecv.at[t, nx - k], x_peer(k))

    def wait_left(t, slots):
        for k in slots:
            wait_bytes((sr, xr)[t].at[k], xrecv.at[t, k])

    def near(index):
        if 0 < index <= len(reaches):
            pl.semaphore_wait(near_sem.at[index - 1], line_count(reaches[index - 1]))
        if index < len(reaches):
            line_signal(near_sem.at[index], reaches[index])

    reaches = [1 << i for i in range(8) if 1 << i < ne - 1]

    def row_grads():
        gate_grad = a_buf[1, 0]
        up_grad = a_buf[2, 0]
        blk = min(256, half_w)

        def piece(col):
            at = pl.ds(pl.multiple_of(col, blk), blk)
            val = lax.dot_general(gate_grad, w_v[0, at, :], COLS_LAST, preferred_element_type=f32)
            val += lax.dot_general(up_grad, w_v[1, at, :], COLS_LAST, preferred_element_type=f32)
            return val.reshape(ne, rows // ne, blk)

        def body(j, carry):
            both = jnp.concatenate([piece(j * blk), piece(half_w + j * blk)], axis=1)
            zs[:, :, pl.ds(pl.multiple_of(j * blk, blk), blk)] = both.astype(bf16)
            return carry

        lax.fori_loop(0, half_w // blk, body, 0)

    def send_rows():
        for k in range(1, ne):
            send(zs.at[lax.rem(me_e + k, ne)], zr.at[ne - k], zsend.at[0], zrecv.at[0], e_peer(k))
        zr[0] = zs[me_e]

    def tokens():
        wait_bytes(zr.at[pl.ds(1, ne - 1)], zrecv.at[0])
        route_load.wait()
        cap = rows // ne
        tall = ne * 2 * cap
        count = token_ref.shape[1]
        route = route_v[0]
        at = ((lax.div(route, cap) - me_e + ne) & (ne - 1)) * (2 * cap) + lax.rem(route, cap)
        col = lax.broadcasted_iota(jnp.int32, (count, tall), 1)
        low = jnp.zeros((count, tall), f32)
        high = jnp.zeros((count, tall), f32)
        for k in range(route.shape[1]):
            low += jnp.where(col == at[:, k : k + 1], 1.0, 0.0)
            high += jnp.where(col == at[:, k : k + 1] + cap, 1.0, 0.0)
        got = zr[...].reshape(tall, half_w)
        token_ref[0, :, :half_w] = jnp.dot(low.astype(bf16), got, preferred_element_type=f32)
        token_ref[0, :, half_w:] = jnp.dot(high.astype(bf16), got, preferred_element_type=f32)

    groups = ((0,), (1, 2))
    st1, st2, st3 = (st1_a, st1_b), (st2_a, st2_b), (st3_a, st3_b)
    c3, yr = (c3_a, c3_b), (yr_a, yr_b)
    known = {t: [] for t in range(3)}

    def product(t, steps):
        left = sr if t == 0 else xr
        fresh = []
        for step in steps:
            fresh += [step] if step in (0, far) else [step, nx - step]
        for k in fresh:
            g_buf[t, k] = lax.dot_general(left[k], a_buf[t, k], ROWS_FIRST, preferred_element_type=f32)

        def read(k, row, col):
            return g_buf[t, k, pl.ds(row, 8), col : col + 128]

        both = known[t] + fresh
        pairs = [(k, l) for at, k in enumerate(both) for l in both[at:] if l in fresh]
        gram_pairs(read, pairs, nx, dx, ff, rows_buf.at[t])
        known[t] = both

    def combine_1(g):
        for at, t in enumerate(groups[g]):
            st1[g][0, at] = gram_tile(rows_buf.at[t])
        for k in order_x:
            send(st1[g].at[0], st1[g].at[nx - k], s1send.at[g], s1recv.at[g], x_peer(k))

    def combine_2(g):
        wait_bytes(st1[g].at[pl.ds(1, nx - 1)], s1recv.at[g])
        parts = dy // 16
        for at, t in enumerate(groups[g]):
            wt_buf[at] = tree_weights(summed_tiles(st1[g], at, nx, True), nx)
            lanes = [wt_buf[at, k : k + 1, :] for k in range(nx)]

            def body(i, carry, at=at, t=t, lanes=lanes):
                src = pl.ds(pl.multiple_of(i * 16, 16), 16)
                dst = pl.ds(pl.multiple_of(lax.rem(i, parts) * 16, 16), 16)
                for c in range(ff // 128):
                    cols = slice(c * 128, c * 128 + 128)
                    total = lanes[0] * g_buf[t, 0, src, cols]
                    for k in range(1, nx):
                        total = total + lanes[k] * g_buf[t, k, src, cols]
                    c3[g][lax.div(i, parts), at, dst, cols] = total.astype(bf16)
                return carry

            lax.fori_loop(0, dx // 16, body, 0)
        for k in order_y:
            send(c3[g].at[lax.rem(me_y + k, ny)], yr[g].at[ny - k], ysend.at[g], yrecv.at[g], y_peer(k))
        yr[g][0] = c3[g][me_y]

    def combine_3(g):
        wait_bytes(yr[g].at[pl.ds(1, ny - 1)], yrecv.at[g])
        pairs = [(k, l) for k in range(ny) for l in range(k, ny)]
        for at, t in enumerate(groups[g]):
            for k in range(ny):
                yf[t, k] = yr[g][k, at].astype(f32)

            def read(k, row, col, t=t):
                return yf[t, k, pl.ds(row, 8), col : col + 128]

            gram_pairs(read, pairs, ny, dy, ff, rows_buf.at[t])
            st2[g][0, at] = gram_tile(rows_buf.at[t])
        for k in order_x:
            send(st2[g].at[0], st2[g].at[nx - k], s2send.at[g], s2recv.at[g], x_peer(k))

    def combine_4(g):
        wait_bytes(st2[g].at[pl.ds(1, nx - 1)], s2recv.at[g])
        for at, t in enumerate(groups[g]):
            st3[g][0, at] = summed_tiles(st2[g], at, nx, False)
        for k in order_y:
            send(st3[g].at[0], st3[g].at[ny - k], s3send.at[g], s3recv.at[g], y_peer(k))

    def combine_5(g):
        wait_bytes(st3[g].at[pl.ds(1, ny - 1)], s3recv.at[g])
        for at, t in enumerate(groups[g]):
            wt_buf[at] = tree_weights(summed_tiles(st3[g], at, ny, True), ny)
            for c in range(ff // 128):
                cols = slice(c * 128, c * 128 + 128)
                total = wt_buf[at, 0:1, :] * yf[t, 0, :, cols]
                for k in range(1, ny):
                    total = total + wt_buf[at, k : k + 1, :] * yf[t, k, :, cols]
                comb_ref[(t + 2) % 3, :, cols] = total

    def steps(tensors, step):
        if step <= far:
            for t in tensors:
                ring_step(t, step)

    near(0)
    steps((1, 2), 1)
    send_left(1, 0)
    row_grads()
    steps((1, 2), 2)
    send_left(1, 1)
    near(1)
    steps((1, 2), 3)
    send_left(1, 2)
    steps((0,), 1)
    near(2)
    steps((1, 2), 4)
    send_left(0, 0)
    wait_left(1, nearest)
    product(1, range(far))
    steps((0,), 2)
    send_left(0, 1)
    product(2, range(far))
    near(3)
    ring_wait(1, far)
    ring_wait(2, far)
    steps((0,), 3)
    send_left(0, 2)
    product(1, [far])
    product(2, [far])
    combine_1(1)
    steps((0,), 4)
    near(4)
    send_rows()
    combine_2(1)
    wait_left(0, nearest[:-1])
    product(0, range(far))
    combine_3(1)
    wait_left(0, nearest[-1:])
    ring_wait(0, far)
    product(0, [far])
    combine_1(0)
    combine_4(1)
    combine_2(0)
    combine_5(1)
    combine_3(0)
    combine_4(0)
    tokens()
    combine_5(0)

    for t, ref in enumerate((sr, xr)):
        wait_bytes(ref.at[pl.ds(1, nx - 1)], xsend.at[t])
    for t in range(3):
        for step in range(1, far + 1):
            for src, dst, at, offset in ring_refs(t, step):
                wait_bytes(src, asend.at[at])
    for g in range(2):
        wait_bytes(st1[g].at[pl.ds(1, nx - 1)], s1send.at[g])
        wait_bytes(yr[g].at[pl.ds(1, ny - 1)], ysend.at[g])
        wait_bytes(st2[g].at[pl.ds(1, nx - 1)], s2send.at[g])
        wait_bytes(st3[g].at[pl.ds(1, ny - 1)], s3send.at[g])
    wait_bytes(zr.at[pl.ds(1, ne - 1)], zsend.at[0])


def on_device(nx, ny, ne, x_rows, row_cot, gate_vals, route_pos, weights, momentum):
    rows, width = x_rows.shape[1:]
    ff = weights.shape[3]
    dx = width // nx
    dy = dx // ny
    far = nx // 2
    tokens = route_pos.shape[1]
    vmem = pltpu.VMEM
    dma = pltpu.SemaphoreType.DMA
    in_hbm = pl.BlockSpec(memory_space=pl.ANY)
    in_vmem = pl.BlockSpec(memory_space=pltpu.VMEM)
    token_sum, combined = pl.pallas_call(
        functools.partial(kernel, nx, ny, ne),
        out_shape=(
            jax.ShapeDtypeStruct((1, tokens, width), f32),
            jax.ShapeDtypeStruct((3, dy, ff), f32),
        ),
        in_specs=[in_hbm] * 5,
        out_specs=(in_vmem, in_vmem),
        scratch_shapes=[
            vmem((rows, width), bf16),
            vmem(gate_vals.shape, f32),
            vmem(route_pos.shape, jnp.int32),
            vmem((3, width, ff), bf16),
            vmem((nx, rows, dx), bf16),
            vmem((nx, rows, dx), bf16),
            vmem((nx, rows, dx), bf16),
            vmem((nx, rows, dx), bf16),
            vmem((3, nx, rows, ff), bf16),
            vmem((3, nx, dx, ff), f32),
            vmem((ne, 2 * rows // ne, width // 2), bf16),
            vmem((ne, 2 * rows // ne, width // 2), bf16),
            vmem((ny, 1, dy, ff), bf16),
            vmem((ny, 2, dy, ff), bf16),
            vmem((ny, 1, dy, ff), bf16),
            vmem((ny, 2, dy, ff), bf16),
            vmem((3, ny, dy, ff), f32),
            vmem((nx, 1, 8, 128), f32),
            vmem((nx, 2, 8, 128), f32),
            vmem((nx, 1, 8, 128), f32),
            vmem((nx, 2, 8, 128), f32),
            vmem((ny, 1, 8, 128), f32),
            vmem((ny, 2, 8, 128), f32),
            vmem((3, 64, 128), f32),
            vmem((2, 8, 128), f32),
            dma((6,)),
            dma((nx,)),
            dma((2,)),
            dma((2, nx)),
            dma((6 * far,)),
            dma((6 * far,)),
            dma((1,)),
            dma((1,)),
            dma((2,)),
            dma((2,)),
            dma((2,)),
            dma((2,)),
            dma((2,)),
            dma((2,)),
            dma((2,)),
            dma((2,)),
            pltpu.SemaphoreType.REGULAR((8,)),
        ],
        compiler_params=pltpu.CompilerParams(
            collective_id=0, has_side_effects=True, vmem_limit_bytes=56 * 1024 * 1024
        ),
        cost_estimate=pl.CostEstimate(
            flops=16 * rows * width * ff, bytes_accessed=2 * (3 * width * ff + 2 * rows * width),
            transcendentals=rows * ff,
        ),
    )(x_rows, row_cot, gate_vals, route_pos, weights)
    token_grad, momentum_new = pl.pallas_call(
        finish,
        out_shape=(
            jax.ShapeDtypeStruct(token_sum.shape, bf16),
            jax.ShapeDtypeStruct(momentum.shape, f32),
        ),
        in_specs=[in_vmem] * 3,
        out_specs=(in_vmem, in_vmem),
    )(token_sum, combined, momentum)
    return (token_grad, momentum_new)


def solution(mesh):
    reps, ne = mesh.shape["rep"], mesh.shape["exp"]
    nx = 1 << ((reps.bit_length()) // 2)
    ny = reps // nx
    placed = (
        P("rep", "exp", None),
        P("rep", "exp", None),
        P("rep", "exp"),
        P("rep", "exp", None),
        P("exp", None, None, None),
        P("exp", None, "rep", None),
    )
    return jax.shard_map(
        functools.partial(on_device, nx, ny, ne),
        mesh=mesh,
        in_specs=placed,
        out_specs=(P("rep", "exp", None), P("exp", None, "rep", None)),
        check_vma=False,
    )
```

```python
import functools
import math

import jax
import jax.numpy as jnp
from jax import lax
from jax.experimental import pallas as pl
from jax.experimental.pallas import tpu as pltpu
from jax.sharding import PartitionSpec as P

MESH = pl.DeviceIdType.MESH
tiny_eps = 1e-06
moment_decay = 0.9
ROWS_FIRST = (((0,), (0,)), ((), ()))
COLS_LAST = (((1,), (1,)), ((), ()))
f32 = jnp.float32
bf16 = jnp.bfloat16


def tile_iotas():
    sub = lax.broadcasted_iota(jnp.int32, (8, 128), 0)
    lane = lax.broadcasted_iota(jnp.int32, (8, 128), 1)
    return sub, lane


def gram_pairs(read, pairs, n, rows, cols, rows_buf):
    used = sorted({k for pair in pairs for k in pair})

    def body(i, accs):
        row = pl.multiple_of(i * 8, 8)
        accs = list(accs)
        for c in range(cols // 128):
            vals = {k: read(k, row, c * 128) for k in used}
            for at, (k, l) in enumerate(pairs):
                accs[at] = accs[at] + vals[k] * vals[l]
        return tuple(accs)

    zero = jnp.zeros((8, 128), f32)
    accs = lax.fori_loop(0, rows // 8, body, tuple(zero for _ in pairs))
    for (k, l), acc in zip(pairs, accs):
        total = jnp.sum(acc, axis=0, keepdims=True)
        for a in range(8):
            for b in range(8):
                if {a % n, b % n} == {k, l}:
                    rows_buf[a * 8 + b : a * 8 + b + 1, :] = total


def gram_tile(rows_buf):
    sub, lane = tile_iotas()
    tile = jnp.zeros((8, 128), f32)
    for b in range(8):
        col = jnp.sum(rows_buf[b * 8 : b * 8 + 8, :], axis=1, keepdims=True)
        tile = tile + jnp.where((lane & 7) == b, col, 0.0)
    return tile


def tree_weights(tile, n):
    sub, lane = tile_iotas()
    weights = jnp.ones((8, 128), f32)
    half = n // 2
    while half >= 1:
        other = (sub + half) & 7
        here_c = jnp.where(lane == sub, tile, 0.0)
        there_c = jnp.where(lane == other, tile, 0.0)
        here_r = jnp.where((lane & 7) == sub, tile, 0.0)
        there_r = jnp.where((lane & 7) == other, tile, 0.0)
        q_col = jnp.maximum(jnp.sum(here_c, axis=1, keepdims=True), 0.0)
        p_col = jnp.sum(there_c, axis=1, keepdims=True)
        q_row = jnp.maximum(jnp.sum(here_r, axis=0, keepdims=True), 0.0)
        p_row = jnp.sum(there_r, axis=0, keepdims=True)
        q_col_b = jnp.broadcast_to(q_col, (8, 128))
        q_row_b = jnp.broadcast_to(q_row, (8, 128))
        most_c = jnp.sqrt(q_col_b) * jnp.sqrt(pltpu.roll(q_col_b, half, 0))
        most_r = jnp.sqrt(q_row_b) * jnp.sqrt(pltpu.roll(q_row_b, half, 1))
        p_col_b = jnp.clip(jnp.broadcast_to(p_col, (8, 128)), -most_c, most_c)
        p_row_b = jnp.clip(jnp.broadcast_to(p_row, (8, 128)), -most_r, most_r)
        coef_c = 1.0 - p_col_b / (2.0 * (q_col_b + tiny_eps))
        coef_r = 1.0 - p_row_b / (2.0 * (q_row_b + tiny_eps))
        weights = weights * coef_c
        tile = tile * coef_c * coef_r
        tile = tile + pltpu.roll(tile, half, 0)
        tile = tile + pltpu.roll(tile, half, 1)
        half //= 2
    return weights


def summed_tiles(buf, at, n, shifted):
    total = buf[0, at]
    for j in range(1, n):
        tile = buf[j, at]
        if shifted:
            tile = pltpu.roll(pltpu.roll(tile, j, 0), j, 1)
        total = total + tile
    return total


def finish(token_ref, comb_ref, mom_ref, token_out, mom_out):
    token_out[...] = token_ref[...].astype(bf16)
    mom_out[0] = moment_decay * mom_ref[0] + (1.0 - moment_decay) * comb_ref[...]


def kernel(
    nx, ny, ne,
    x_ref, cot_ref, gate_ref, route_ref, w_ref,
    token_ref, comb_ref,
    cot_v, gate_v, route_v, w_v, xs, ss, xr, sr, a_buf, g_buf, zs, zr,
    c3_a, c3_b, yr_a, yr_b, yf, st1_a, st1_b, st2_a, st2_b, st3_a, st3_b, rows_buf, wt_buf,
    load_sem, x_sem, xsend, xrecv, asend, arecv, zsend, zrecv,
    ysend, yrecv, s1send, s1recv, s2send, s2recv, s3send, s3recv, near_sem,
):
    rep = lax.axis_index("rep")
    me_e = lax.axis_index("exp")
    me_x = lax.div(rep, ny)
    me_y = lax.rem(rep, ny)
    rows, width = cot_v.shape
    ff = w_v.shape[2]
    dx = width // nx
    dy = dx // ny
    half_w = width // 2
    far = nx // 2

    def x_peer(k):
        return (lax.rem(me_x + k, nx) * ny + me_y, me_e)

    def y_peer(k):
        return (me_x * ny + lax.rem(me_y + k, ny), me_e)

    def e_peer(k):
        return (rep, lax.rem(me_e + k, ne))

    chips = ne // 2
    chip = lax.div(me_e, 2)
    place = jnp.where(lax.rem(me_e, 2) == 0, chip, ne - 1 - chip)

    def on_line(at):
        return (rep, jnp.where(at < chips, 2 * at, 2 * (ne - 1 - at) + 1))

    def line_signal(sem, reach):
        @pl.when(place >= reach)
        def _():
            pl.semaphore_signal(sem, inc=1, device_id=on_line(place - reach), device_id_type=MESH)

        @pl.when(place + reach < ne)
        def _():
            pl.semaphore_signal(sem, inc=1, device_id=on_line(place + reach), device_id_type=MESH)

    def line_count(reach):
        return (place >= reach).astype(jnp.int32) + (place + reach < ne).astype(jnp.int32)

    cot_load = pltpu.make_async_copy(cot_ref.at[0], cot_v, load_sem.at[0])
    cot_load.start()
    gate_load = pltpu.make_async_copy(gate_ref, gate_v, load_sem.at[4])
    gate_load.start()
    x_loads = []
    for j in range(nx):
        load = pltpu.make_async_copy(x_ref.at[0, :, pl.ds(j * dx, dx)], xs.at[j], x_sem.at[j])
        load.start()
        x_loads.append(load)
    w_loads = []
    for t in range(3):
        load = pltpu.make_async_copy(w_ref.at[0, t], w_v.at[t], load_sem.at[1 + t])
        load.start()
        w_loads.append(load)
    route_load = pltpu.make_async_copy(route_ref, route_v, load_sem.at[5])
    route_load.start()

    barrier = pltpu.get_barrier_semaphore()
    peers = [x_peer(k) for k in range(1, nx)]
    peers += [y_peer(k) for k in range(1, ny)]
    for peer in peers:
        pl.semaphore_signal(barrier, inc=1, device_id=peer, device_id_type=MESH)

    line_signal(barrier, 1)

    eye = lax.broadcasted_iota(jnp.int32, (rows, rows), 0) == lax.broadcasted_iota(
        jnp.int32, (rows, rows), 1
    )
    cot_load.wait()
    gate_load.wait()
    gate_col = jnp.sum(jnp.where(eye, gate_v[...], 0.0), axis=1, keepdims=True)
    for j in range(nx):
        ss[j] = (gate_col * cot_v[:, j * dx : (j + 1) * dx].astype(f32)).astype(bf16)

    for load in x_loads:
        load.wait()
    w_loads[0].wait()
    w_loads[1].wait()
    gate_pre = jnp.zeros((rows, ff), f32)
    up_pre = jnp.zeros((rows, ff), f32)
    for j in range(nx):
        part = xs[j]
        gate_pre += jnp.dot(part, w_v[0, j * dx : (j + 1) * dx, :], preferred_element_type=f32)
        up_pre += jnp.dot(part, w_v[1, j * dx : (j + 1) * dx, :], preferred_element_type=f32)
    sigma = 1.0 / (1.0 + jnp.exp(-gate_pre))
    act = gate_pre * sigma
    a_buf[0, 0] = (act * up_pre).astype(bf16)
    w_loads[2].wait()
    hidden_grad = jnp.zeros((rows, ff), f32)
    for j in range(nx):
        hidden_grad += jnp.dot(ss[j], w_v[2, j * dx : (j + 1) * dx, :], preferred_element_type=f32)
    a_buf[1, 0] = (hidden_grad * up_pre * sigma * (1.0 + gate_pre * (1.0 - sigma))).astype(bf16)
    a_buf[2, 0] = (hidden_grad * act).astype(bf16)
    sr[0] = ss[me_x]
    xr[0] = xs[me_x]

    pl.semaphore_wait(barrier, len(peers) + line_count(1))

    def send(src, dst, ssem, rsem, peer):
        copy = pltpu.make_async_remote_copy(
            src_ref=src, dst_ref=dst, send_sem=ssem, recv_sem=rsem,
            device_id=peer, device_id_type=MESH,
        )
        copy.start()

    def wait_bytes(ref, sem):
        pltpu.make_async_copy(ref, ref, sem).wait()

    order_x = sorted(range(1, nx), key=lambda k: -min(k, nx - k))
    order_y = sorted(range(1, ny), key=lambda k: -min(k, ny - k))

    def ring_parts(step):
        parts = []
        if step < far:
            parts.append(((nx - step + 1) % nx, nx - step, 0, rows, 1))
            parts.append((step - 1, step, 0, rows, nx - 1))
        else:
            parts.append(((nx - step + 1) % nx, far, 0, rows // 2, 1))
            parts.append((step - 1, far, rows // 2, rows // 2, nx - 1))
        return parts

    def ring_refs(t, step):
        found = []
        for way, (src, dst, first, count, offset) in enumerate(ring_parts(step)):
            found.append((
                a_buf.at[t, src, pl.ds(first, count)],
                a_buf.at[t, dst, pl.ds(first, count)],
                (t * far + step - 1) * 2 + way,
                offset,
            ))
        return found

    def ring_wait(t, step):
        for src, dst, at, offset in ring_refs(t, step):
            wait_bytes(dst, arecv.at[at])

    def ring_step(t, step):
        if step > 1:
            ring_wait(t, step - 1)
        for src, dst, at, offset in ring_refs(t, step):
            send(src, dst, asend.at[at], arecv.at[at], x_peer(offset))

    nearest = []
    for k in range(1, far):
        nearest += [k, nx - k]
    nearest.append(far)
    cuts = (0, (len(nearest) + 1) * 3 // 8, (len(nearest) + 1) * 5 // 8, len(nearest))

    def send_left(t, piece):
        mine, there = (ss, sr) if t == 0 else (xs, xr)
        for k in nearest[cuts[piece] : cuts[piece + 1]]:
            send(mine.at[lax.rem(me_x + k, nx)], there.at[nx - k], xsend.at[t], xrecv.at[t, nx - k], x_peer(k))

    def wait_left(t, slots):
        for k in slots:
            wait_bytes((sr, xr)[t].at[k], xrecv.at[t, k])

    def near(index):
        if 0 < index <= len(reaches):
            pl.semaphore_wait(near_sem.at[index - 1], line_count(reaches[index - 1]))
        if index < len(reaches):
            line_signal(near_sem.at[index], reaches[index])

    reaches = [1 << i for i in range(8) if 1 << i < ne - 1]

    def row_grads():
        gate_grad = a_buf[1, 0]
        up_grad = a_buf[2, 0]
        blk = min(256, half_w)

        def piece(col):
            at = pl.ds(pl.multiple_of(col, blk), blk)
            val = lax.dot_general(gate_grad, w_v[0, at, :], COLS_LAST, preferred_element_type=f32)
            val += lax.dot_general(up_grad, w_v[1, at, :], COLS_LAST, preferred_element_type=f32)
            return val.reshape(ne, rows // ne, blk)

        def body(j, carry):
            both = jnp.concatenate([piece(j * blk), piece(half_w + j * blk)], axis=1)
            zs[:, :, pl.ds(pl.multiple_of(j * blk, blk), blk)] = both.astype(bf16)
            return carry

        lax.fori_loop(0, half_w // blk, body, 0)

    def send_rows():
        for k in range(1, ne):
            send(zs.at[lax.rem(me_e + k, ne)], zr.at[ne - k], zsend.at[0], zrecv.at[0], e_peer(k))
        zr[0] = zs[me_e]

    def tokens():
        wait_bytes(zr.at[pl.ds(1, ne - 1)], zrecv.at[0])
        route_load.wait()
        cap = rows // ne
        tall = ne * 2 * cap
        count = token_ref.shape[1]
        route = route_v[0]
        at = ((lax.div(route, cap) - me_e + ne) & (ne - 1)) * (2 * cap) + lax.rem(route, cap)
        row = lax.broadcasted_iota(jnp.int32, (tall, count), 0)
        low = jnp.zeros((tall, count), f32)
        high = jnp.zeros((tall, count), f32)
        for k in range(route.shape[0]):
            low += jnp.where(row == at[k : k + 1, :], 1.0, 0.0)
            high += jnp.where(row == at[k : k + 1, :] + cap, 1.0, 0.0)
        got = zr[...].reshape(tall, half_w)
        for picks, cols in ((low, slice(0, half_w)), (high, slice(half_w, width))):
            token_ref[0, :, cols] = lax.dot_general(
                picks.astype(bf16), got, ROWS_FIRST, preferred_element_type=f32
            )

    groups = ((0,), (1, 2))
    st1, st2, st3 = (st1_a, st1_b), (st2_a, st2_b), (st3_a, st3_b)
    c3, yr = (c3_a, c3_b), (yr_a, yr_b)
    known = {t: [] for t in range(3)}

    def product(t, steps):
        left = sr if t == 0 else xr
        fresh = []
        for step in steps:
            fresh += [step] if step in (0, far) else [step, nx - step]
        for k in fresh:
            g_buf[t, k] = lax.dot_general(left[k], a_buf[t, k], ROWS_FIRST, preferred_element_type=f32)

        def read(k, row, col):
            return g_buf[t, k, pl.ds(row, 8), col : col + 128]

        both = known[t] + fresh
        pairs = [(k, l) for at, k in enumerate(both) for l in both[at:] if l in fresh]
        gram_pairs(read, pairs, nx, dx, ff, rows_buf.at[t])
        known[t] = both

    def combine_1(g):
        for at, t in enumerate(groups[g]):
            st1[g][0, at] = gram_tile(rows_buf.at[t])
        for k in order_x:
            send(st1[g].at[0], st1[g].at[nx - k], s1send.at[g], s1recv.at[g], x_peer(k))

    def combine_2(g):
        wait_bytes(st1[g].at[pl.ds(1, nx - 1)], s1recv.at[g])
        parts = dy // 16
        for at, t in enumerate(groups[g]):
            wt_buf[at] = tree_weights(summed_tiles(st1[g], at, nx, True), nx)
            lanes = [wt_buf[at, k : k + 1, :] for k in range(nx)]

            def body(i, carry, at=at, t=t, lanes=lanes):
                src = pl.ds(pl.multiple_of(i * 16, 16), 16)
                dst = pl.ds(pl.multiple_of(lax.rem(i, parts) * 16, 16), 16)
                for c in range(ff // 128):
                    cols = slice(c * 128, c * 128 + 128)
                    total = lanes[0] * g_buf[t, 0, src, cols]
                    for k in range(1, nx):
                        total = total + lanes[k] * g_buf[t, k, src, cols]
                    c3[g][lax.div(i, parts), at, dst, cols] = total.astype(bf16)
                return carry

            lax.fori_loop(0, dx // 16, body, 0)
        for k in order_y:
            send(c3[g].at[lax.rem(me_y + k, ny)], yr[g].at[ny - k], ysend.at[g], yrecv.at[g], y_peer(k))
        yr[g][0] = c3[g][me_y]

    def combine_3(g):
        wait_bytes(yr[g].at[pl.ds(1, ny - 1)], yrecv.at[g])
        pairs = [(k, l) for k in range(ny) for l in range(k, ny)]
        for at, t in enumerate(groups[g]):
            for k in range(ny):
                yf[t, k] = yr[g][k, at].astype(f32)

            def read(k, row, col, t=t):
                return yf[t, k, pl.ds(row, 8), col : col + 128]

            gram_pairs(read, pairs, ny, dy, ff, rows_buf.at[t])
            st2[g][0, at] = gram_tile(rows_buf.at[t])
        for k in order_x:
            send(st2[g].at[0], st2[g].at[nx - k], s2send.at[g], s2recv.at[g], x_peer(k))

    def combine_4(g):
        wait_bytes(st2[g].at[pl.ds(1, nx - 1)], s2recv.at[g])
        for at, t in enumerate(groups[g]):
            st3[g][0, at] = summed_tiles(st2[g], at, nx, False)
        for k in order_y:
            send(st3[g].at[0], st3[g].at[ny - k], s3send.at[g], s3recv.at[g], y_peer(k))

    def combine_5(g):
        wait_bytes(st3[g].at[pl.ds(1, ny - 1)], s3recv.at[g])
        for at, t in enumerate(groups[g]):
            wt_buf[at] = tree_weights(summed_tiles(st3[g], at, ny, True), ny)
            for c in range(ff // 128):
                cols = slice(c * 128, c * 128 + 128)
                total = wt_buf[at, 0:1, :] * yf[t, 0, :, cols]
                for k in range(1, ny):
                    total = total + wt_buf[at, k : k + 1, :] * yf[t, k, :, cols]
                comb_ref[(t + 2) % 3, :, cols] = total

    def steps(tensors, step):
        if step <= far:
            for t in tensors:
                ring_step(t, step)

    near(0)
    steps((1, 2, 0), 1)
    for piece in range(3):
        send_left(1, piece)
    send_left(0, 0)
    row_grads()
    near(1)
    steps((1, 2, 0), 2)
    send_left(0, 1)
    send_left(0, 2)
    near(2)
    steps((1, 2, 0), 3)
    wait_left(1, nearest)
    product(1, range(far - 1))
    product(2, range(far - 1))
    wait_left(0, nearest)
    product(0, range(far - 1))
    near(3)
    steps((1, 2, 0), 4)
    product(1, [far - 1])
    product(2, [far - 1])
    product(0, [far - 1])
    ring_wait(1, far)
    ring_wait(2, far)
    product(1, [far])
    product(2, [far])
    combine_1(1)
    ring_wait(0, far)
    product(0, [far])
    combine_1(0)
    near(4)
    send_rows()
    combine_2(1)
    combine_2(0)
    combine_3(1)
    combine_3(0)
    combine_4(1)
    combine_4(0)
    combine_5(1)
    tokens()
    for t, ref in enumerate((sr, xr)):
        wait_bytes(ref.at[pl.ds(1, nx - 1)], xsend.at[t])
    for t in range(3):
        for step in range(1, far + 1):
            for src, dst, at, offset in ring_refs(t, step):
                wait_bytes(src, asend.at[at])
    for g in range(2):
        wait_bytes(st1[g].at[pl.ds(1, nx - 1)], s1send.at[g])
        wait_bytes(yr[g].at[pl.ds(1, ny - 1)], ysend.at[g])
        wait_bytes(st2[g].at[pl.ds(1, nx - 1)], s2send.at[g])
        wait_bytes(st3[g].at[pl.ds(1, ny - 1)], s3send.at[g])
    wait_bytes(zr.at[pl.ds(1, ne - 1)], zsend.at[0])
    combine_5(0)


def on_device(nx, ny, ne, x_rows, row_cot, gate_vals, route_pos, weights, momentum):
    rows, width = x_rows.shape[1:]
    ff = weights.shape[3]
    dx = width // nx
    dy = dx // ny
    far = nx // 2
    tokens = route_pos.shape[1]
    by_choice = jnp.swapaxes(route_pos, 1, 2)
    vmem = pltpu.VMEM
    dma = pltpu.SemaphoreType.DMA
    in_hbm = pl.BlockSpec(memory_space=pl.ANY)
    in_vmem = pl.BlockSpec(memory_space=pltpu.VMEM)
    token_sum, combined = pl.pallas_call(
        functools.partial(kernel, nx, ny, ne),
        out_shape=(
            jax.ShapeDtypeStruct((1, tokens, width), f32),
            jax.ShapeDtypeStruct((3, dy, ff), f32),
        ),
        in_specs=[in_hbm] * 5,
        out_specs=(in_vmem, in_vmem),
        scratch_shapes=[
            vmem((rows, width), bf16),
            vmem(gate_vals.shape, f32),
            vmem(by_choice.shape, jnp.int32),
            vmem((3, width, ff), bf16),
            vmem((nx, rows, dx), bf16),
            vmem((nx, rows, dx), bf16),
            vmem((nx, rows, dx), bf16),
            vmem((nx, rows, dx), bf16),
            vmem((3, nx, rows, ff), bf16),
            vmem((3, nx, dx, ff), f32),
            vmem((ne, 2 * rows // ne, width // 2), bf16),
            vmem((ne, 2 * rows // ne, width // 2), bf16),
            vmem((ny, 1, dy, ff), bf16),
            vmem((ny, 2, dy, ff), bf16),
            vmem((ny, 1, dy, ff), bf16),
            vmem((ny, 2, dy, ff), bf16),
            vmem((3, ny, dy, ff), f32),
            vmem((nx, 1, 8, 128), f32),
            vmem((nx, 2, 8, 128), f32),
            vmem((nx, 1, 8, 128), f32),
            vmem((nx, 2, 8, 128), f32),
            vmem((ny, 1, 8, 128), f32),
            vmem((ny, 2, 8, 128), f32),
            vmem((3, 64, 128), f32),
            vmem((2, 8, 128), f32),
            dma((6,)),
            dma((nx,)),
            dma((2,)),
            dma((2, nx)),
            dma((6 * far,)),
            dma((6 * far,)),
            dma((1,)),
            dma((1,)),
            dma((2,)),
            dma((2,)),
            dma((2,)),
            dma((2,)),
            dma((2,)),
            dma((2,)),
            dma((2,)),
            dma((2,)),
            pltpu.SemaphoreType.REGULAR((8,)),
        ],
        compiler_params=pltpu.CompilerParams(
            collective_id=0, has_side_effects=True, vmem_limit_bytes=56 * 1024 * 1024
        ),
        cost_estimate=pl.CostEstimate(
            flops=16 * rows * width * ff, bytes_accessed=2 * (3 * width * ff + 2 * rows * width),
            transcendentals=rows * ff,
        ),
    )(x_rows, row_cot, gate_vals, by_choice, weights)
    token_grad, momentum_new = pl.pallas_call(
        finish,
        out_shape=(
            jax.ShapeDtypeStruct(token_sum.shape, bf16),
            jax.ShapeDtypeStruct(momentum.shape, f32),
        ),
        in_specs=[in_vmem] * 3,
        out_specs=(in_vmem, in_vmem),
    )(token_sum, combined, momentum)
    return (token_grad, momentum_new)


def solution(mesh):
    reps, ne = mesh.shape["rep"], mesh.shape["exp"]
    nx = 1 << ((reps.bit_length()) // 2)
    ny = reps // nx
    placed = (
        P("rep", "exp", None),
        P("rep", "exp", None),
        P("rep", "exp"),
        P("rep", "exp", None),
        P("exp", None, None, None),
        P("exp", None, "rep", None),
    )
    return jax.shard_map(
        functools.partial(on_device, nx, ny, ne),
        mesh=mesh,
        in_specs=placed,
        out_specs=(P("rep", "exp", None), P("exp", None, "rep", None)),
        check_vma=False,
    )
```
